32 devices in a mesh: ctx: 8 (over z, x), pp: 4 (over y, core).
Axes of the slice: x: 2, y: 2, z: 4, core: 2. Of those that a mesh axis runs over, the one named last changes fastest.
Arguments:
- tokens: bfloat16 [1, 1024, 2048], P(None, 'ctx'), may hold values from -6 to 6
- doc_lengths: int32 [4], replicated, may hold values from 1 to 512, 1024 in all
- norm_gain: bfloat16 [4, 2048], P('pp'), may hold values from 0.25 to 1.75
- w_query: bfloat16 [4, 2048, 2048], P('pp'), as said below
- w_key: bfloat16 [4, 2048, 512], P('pp'), as said below
- w_value: bfloat16 [4, 2048, 512], P('pp'), may hold values from -0.125 to 0.125
- w_output: bfloat16 [4, 2048, 2048], P('pp'), may hold values from -0.125 to 0.125
Outputs:
- section_states: bfloat16 [4, 1, 1024, 2048], P('pp', None, 'ctx')
The draws below stay inside these ranges and needn't reach their ends.
Inputs may be any that keep to these rules, and one draw needn't show every extreme that they name: `doc_lengths`: document lengths sum to 1024; the longest is exactly 512. `w_query`: entries lie within 6 / sqrt(2048) of zero. `w_key`: entries lie within 6 / sqrt(2048) of zero.
All inputs are finite; a program needn't handle non-finite values.
Results may differ from the reference program's by a relative error of at most 0.014.
The reference program's roundings to bfloat16 on the way count: a program that leaves them out, or rounds other values in their place, can miss the bound.
Values may be sent and summed in bfloat16 or wider, within the bound.
A program may use at most 192 MiB of HBM per device.

```python
import math
import jax
import jax.numpy as jnp
import numpy as np
from jax import lax

D = 2048
HD = 128
HQ = 16
KV = 4
TOK_DEV = 128
MICRO = 1
TOKENS = 1024
DOCS = 4
SECTIONS = 4
N_CTX = 8
N_PP = 4


def drawn_weights(key, salt, columns):
    noise_key = jax.random.fold_in(key, salt)
    full_shape = (SECTIONS, D, columns)
    inverse_root = 1.0 / math.sqrt(D)
    drawn = jax.random.truncated_normal(noise_key, -6.0, 6.0, full_shape, jnp.float32)
    return (drawn * inverse_root).astype(jnp.bfloat16)


def draw_tokens(key, part):
    full_shape = (MICRO, TOKENS, D)
    entries = jax.random.truncated_normal(jax.random.fold_in(key, 21), -6.0, 6.0, full_shape, jnp.float32)
    return entries.astype(jnp.bfloat16)


def draw_w_query(key, part):
    return drawn_weights(key, 11, HQ * HD)


def draw_w_key(key, part):
    return drawn_weights(key, 12, KV * HD)


def levels(key, shape, cuts, low, high):
    level = 1.0
    for position, blocks in cuts:
        heights = jax.random.uniform(jax.random.fold_in(jax.random.fold_in(key, 6), position), (blocks,), jnp.float32, low / len(cuts), high / len(cuts))
        level = level * jnp.repeat(jnp.exp(heights), shape[position] // blocks).reshape((-1,) + (1,) * (len(shape) - 1 - position))
    return level


def length_profile(amount, total, limit, lean):
    loads = [(1 << 20) // math.isqrt(rank ** lean) + 1 for rank in range(2, amount + 1)]
    surplus, given = total - limit - (amount - 1), [1] * (amount - 1)
    while surplus > 0:
        free = [i for i in range(amount - 1) if given[i] < limit]
        pool, left = sum([loads[i] for i in free]), surplus
        for i in free:
            extra = min(limit - given[i], max(1, left * loads[i] // pool), surplus)
            given[i] = given[i] + extra
            surplus = surplus - extra
    return np.array([limit] + given)


def ragged_sizes(rng, amount, total, bound, slope):
    if amount == 2:
        one = jax.random.randint(rng, (), max(1, total - bound), min(bound, total - 1) + 1)
        return jnp.stack([one, total - one])
    sizes = jnp.asarray(length_profile(amount, total, bound, slope), jnp.int32)
    twos = (amount - 1) // 2
    source_of, sink = sizes[1:1 + 2 * twos:2], sizes[2:2 + 2 * twos:2]
    room = jnp.minimum(source_of - 1, bound - sink)
    passed = jax.random.randint(jax.random.fold_in(rng, 1), (twos,), 0, 1 << 20) % (room + 1)
    sizes = sizes.at[1:1 + 2 * twos:2].set(source_of - passed).at[2:2 + 2 * twos:2].set(sink + passed)
    return sizes[jax.random.permutation(jax.random.fold_in(rng, 2), amount)]


def gaussian(stream_key, dims, scale, most, cuts=(), kind=jnp.bfloat16):
    result = jax.random.normal(stream_key, dims, jnp.float32) * scale
    if len(cuts) > 0:
        result = levels(stream_key, dims, cuts, -0.22, 0.18) * result
    return jnp.clip(result, min=-most, max=most).astype(kind)


def setup_inputs(seed: int = 0) -> dict:
    key_list = jax.random.split(jax.random.key(seed), 8)
    tokens = draw_tokens(jax.random.fold_in(key_list[7], 71), 0)
    doc_lengths = ragged_sizes(key_list[1], DOCS, TOKENS, TOKENS // 2, 2).astype(jnp.int32)
    norm_gain = jnp.clip(1.0 + 0.15 * jax.random.normal(key_list[2], (SECTIONS, D), jnp.float32), 0.25, 1.75).astype(jnp.bfloat16)
    w_query = draw_w_query(jax.random.fold_in(key_list[7], 71), 0)
    w_key = draw_w_key(jax.random.fold_in(key_list[7], 71), 0)
    w_value = gaussian(key_list[5], (SECTIONS, D, KV * HD), D ** -0.5, 0.125, ((0, 4),))
    w_output = gaussian(key_list[6], (SECTIONS, HQ * HD, D), (HQ * HD) ** -0.5, 0.125, ((0, 4),))
    return {"tokens": tokens, "doc_lengths": doc_lengths, "norm_gain": norm_gain, "w_query": w_query, "w_key": w_key, "w_value": w_value, "w_output": w_output}


THETA = 500000.0
EPSILON = 1e-05
NEG_LARGE = -1e+30

def doc_of(positions, lengths):
    ends = jnp.cumsum(lengths).astype(jnp.int32)
    before = ends[None, :] <= positions[:, None]
    doc_ids = lax.optimization_barrier(jnp.sum(before.astype(jnp.int32), axis=1)).astype(jnp.int32)
    starts = lax.optimization_barrier(jnp.sum(jnp.where(before, lengths[None, :], 0), axis=1)).astype(jnp.int32)
    return (doc_ids, starts)

def rotate(vectors, offsets):
    half = vectors.shape[-1] // 2
    freqs = THETA ** (-(jnp.arange(half, dtype=jnp.float32) * 2.0 / vectors.shape[-1]))
    angles = offsets.astype(jnp.float32)[:, None] * freqs[None, :]
    cosine = jnp.cos(angles)[:, None, :]
    sine = jnp.sin(angles)[:, None, :]
    first = vectors[..., :half]
    second = vectors[..., half:]
    return jnp.concatenate([first * cosine - second * sine, second * cosine + first * sine], axis=-1)

def project(hidden, gain, w_query, w_key, w_value, offsets):
    wide = hidden.astype(jnp.float32)
    normed = (wide * lax.rsqrt(lax.optimization_barrier(jnp.mean(wide * wide, axis=-1, keepdims=True)) + EPSILON) * gain.astype(jnp.float32)).astype(jnp.bfloat16)
    count = hidden.shape[0]
    queries = jnp.dot(normed, w_query, preferred_element_type=jnp.float32).reshape(count, -1, HD)
    queries = rotate(queries, offsets).astype(jnp.bfloat16)
    keys = jnp.dot(normed, w_key, preferred_element_type=jnp.float32).reshape(count, -1, HD)
    keys = rotate(keys, offsets).astype(jnp.bfloat16)
    values = jnp.dot(normed, w_value, preferred_element_type=jnp.float32).astype(jnp.bfloat16)
    return (queries, keys, values)

def section(hidden, lengths, gain, w_query, w_key, w_value, w_output):
    positions = jnp.arange(TOKENS, dtype=jnp.int32)
    doc_ids, starts = doc_of(positions, lengths)
    queries, keys, values = project(hidden, gain, w_query, w_key, w_value, positions - starts)
    keys32 = keys.astype(jnp.float32)
    values32 = values.astype(jnp.float32).reshape(TOKENS, KV, HD)
    scale = HD ** (-0.5)
    group = HQ // KV

    def block(items):
        block_q, block_ids, block_pos = items
        grouped = block_q.astype(jnp.float32).reshape(TOK_DEV, KV, group, HD)
        scores = jnp.einsum('qgjd,kgd->gjqk', grouped, keys32) * scale
        allowed = (doc_ids[None, :] == block_ids[:, None]) & (positions[None, :] <= block_pos[:, None])
        scores = jnp.where(allowed[None, None], scores, NEG_LARGE)
        peak = lax.optimization_barrier(jnp.max(scores, axis=-1, keepdims=True))
        weights = jnp.where(allowed[None, None], jnp.exp(scores - peak), 0.0)
        total = lax.optimization_barrier(jnp.sum(weights, axis=-1))
        mixed = jnp.einsum('gjqk,kgd->gjqd', weights.astype(jnp.bfloat16).astype(jnp.float32), values32)
        mixed = (mixed / total[..., None]).reshape(HQ, TOK_DEV, HD)
        return jnp.transpose(mixed, (1, 0, 2)).reshape(TOK_DEV, HQ * HD).astype(jnp.bfloat16)
    attended = lax.map(block, (queries.reshape(N_CTX, TOK_DEV, HQ, HD), doc_ids.reshape(N_CTX, TOK_DEV), positions.reshape(N_CTX, TOK_DEV)))
    attended = attended.reshape(TOKENS, HQ * HD)
    return (hidden.astype(jnp.float32) + jnp.dot(attended, w_output, preferred_element_type=jnp.float32)).astype(jnp.bfloat16)

def reference(tokens, doc_lengths, norm_gain, w_query, w_key, w_value, w_output):
    results = []
    for segment in range(N_PP):
        row = []
        for micro_index in range(MICRO):
            source = tokens[micro_index] if segment == 0 else results[segment - 1][micro_index]
            row.append(section(source, doc_lengths, norm_gain[segment], w_query[segment], w_key[segment], w_value[segment], w_output[segment]))
        results.append(row)
    return jnp.stack([jnp.stack(row) for row in results])
```

```python
import jax
import jax.numpy as jnp
from jax import lax
from jax.sharding import PartitionSpec as P

HD = 128


THETA = 500000.0
EPSILON = 1e-05
NEG_LARGE = -1e30


def shifted(value, axis, by):
    count = lax.axis_size(axis)
    pairs = [(i, i + by) for i in range(count) if 0 <= i + by < count]
    return lax.ppermute(value, axis, pairs)


def doc_of(positions, lengths):
    order = jnp.arange(lengths.shape[0], dtype=jnp.int32)
    ends = jnp.sum(jnp.where(order[None, :] <= order[:, None], lengths[None, :], 0), axis=1)
    before = ends[None, :] <= positions[:, None]
    doc_ids = jnp.sum(before.astype(jnp.int32), axis=1)
    starts = jnp.sum(jnp.where(before, lengths[None, :], 0), axis=1)
    return (doc_ids, starts)


def rotate(vectors, offsets):
    half = vectors.shape[-1] // 2
    freqs = THETA ** (-(jnp.arange(half, dtype=jnp.float32) * 2.0 / vectors.shape[-1]))
    angles = offsets.astype(jnp.float32)[:, None] * freqs[None, :]
    cosine = jnp.cos(angles)[:, None, :]
    sine = jnp.sin(angles)[:, None, :]
    first = vectors[..., :half]
    second = vectors[..., half:]
    return jnp.concatenate(
        [first * cosine - second * sine, second * cosine + first * sine], axis=-1
    )


def project(hidden, gain, w_query, w_key, w_value, offsets):
    wide = hidden.astype(jnp.float32)
    normed = (
        wide
        * lax.rsqrt(jnp.mean(wide * wide, axis=-1, keepdims=True) + EPSILON)
        * gain.astype(jnp.float32)
    ).astype(jnp.bfloat16)
    count = hidden.shape[0]
    queries = jnp.dot(normed, w_query, preferred_element_type=jnp.float32).reshape(count, -1, HD)
    queries = rotate(queries, offsets).astype(jnp.bfloat16)
    keys = jnp.dot(normed, w_key, preferred_element_type=jnp.float32).reshape(count, -1, HD)
    keys = rotate(keys, offsets).astype(jnp.bfloat16)
    values = jnp.dot(normed, w_value, preferred_element_type=jnp.float32).astype(jnp.bfloat16)
    return (queries, keys, values)


def section(
    hidden, lengths, gain, w_query, w_key, w_value, w_output, query_pos, query_ids, offsets
):
    rows = hidden.shape[0]
    queries, keys, values = project(hidden, gain, w_query, w_key, w_value, offsets)
    heads = queries.shape[1]
    kv_heads = keys.shape[1]
    group = heads // kv_heads
    grouped = queries.reshape(rows, kv_heads, group, HD)
    scale = HD ** (-0.5)
    stacked = jnp.stack([keys.reshape(rows, kv_heads * HD), values])
    piece = lax.all_gather(stacked, "ctx", axis=1, tiled=True)
    peak = jnp.full((kv_heads, group, rows), NEG_LARGE, jnp.float32)
    count = piece.shape[1]
    key_pos = jnp.arange(count, dtype=jnp.int32)
    key_ids, unused = doc_of(key_pos, lengths)
    allowed = (
        (key_ids[None, :] == query_ids[:, None])
        & (key_pos[None, :] <= query_pos[:, None])
        & (key_pos[None, :] >= 0)
    )
    piece_keys = piece[0].reshape(count, kv_heads, HD)
    piece_values = piece[1].reshape(count, kv_heads, HD)
    scores = (
        jnp.einsum("qgjd,kgd->gjqk", grouped, piece_keys, preferred_element_type=jnp.float32)
        * scale
    )
    scores = jnp.where(allowed[None, None], scores, NEG_LARGE)
    new_peak = jnp.maximum(peak, jnp.max(scores, axis=-1))
    weights = jnp.where(allowed[None, None], jnp.exp(scores - new_peak[..., None]), 0.0)
    total = jnp.sum(weights, axis=-1)
    accum = jnp.einsum(
        "gjqk,kgd->gjqd",
        weights.astype(jnp.bfloat16),
        piece_values,
        preferred_element_type=jnp.float32,
    )
    state = (new_peak, total, accum)
    peak, total, accum = state
    mixed = (accum / total[..., None]).reshape(heads, rows, HD)
    attended = jnp.transpose(mixed, (1, 0, 2)).reshape(rows, heads * HD).astype(jnp.bfloat16)
    return (
        hidden.astype(jnp.float32) + jnp.dot(attended, w_output, preferred_element_type=jnp.float32)
    ).astype(jnp.bfloat16)


def per_device(tokens, doc_lengths, norm_gain, w_query, w_key, w_value, w_output):
    micro_count = tokens.shape[0]
    rows = tokens.shape[1]
    segment = lax.axis_index("pp")
    span_index = lax.axis_index("ctx")
    query_pos = span_index * rows + jnp.arange(rows, dtype=jnp.int32)
    query_ids, starts = doc_of(query_pos, doc_lengths)
    offsets = query_pos - starts
    ticks = micro_count + lax.axis_size("pp") - 1
    incoming = jnp.zeros((rows, tokens.shape[2]), jnp.bfloat16)
    results = jnp.zeros(tokens.shape, jnp.bfloat16)
    for tick in range(ticks):
        own = tokens[min(tick, micro_count - 1)]
        source = jnp.where(segment == 0, own, incoming)
        output = section(
            source,
            doc_lengths,
            norm_gain[0],
            w_query[0],
            w_key[0],
            w_value[0],
            w_output[0],
            query_pos,
            query_ids,
            offsets,
        )
        micro_index = tick - segment
        slot = jnp.clip(micro_index, 0, micro_count - 1)
        valid = (micro_index >= 0) & (micro_index < micro_count)
        current = lax.dynamic_index_in_dim(results, slot, 0, keepdims=False)
        chosen = jnp.where(valid, output, current)
        results = chosen[None]
        if tick + 1 < ticks:
            incoming = shifted(output, "pp", 1)
    return results[None]


def solution(mesh):
    in_specs = (
        P(None, "ctx", None),
        P(),
        P("pp", None),
        P("pp", None, None),
        P("pp", None, None),
        P("pp", None, None),
        P("pp", None, None),
    )
    out_specs = P("pp", None, "ctx", None)
    return jax.shard_map(
        per_device, mesh=mesh, in_specs=in_specs, out_specs=out_specs, check_vma=False
    )
```

```python
import functools

import jax
import jax.numpy as jnp
from jax import lax
from jax.experimental import pallas as pl
from jax.experimental.pallas import tpu as pltpu
from jax.sharding import PartitionSpec as P

HD = 128
THETA = 500000.0
EPSILON = 1e-05
NEG_LARGE = -1e30
MESH = pl.DeviceIdType.MESH


def tables(position, lengths):
    order = jnp.arange(lengths.shape[0], dtype=jnp.int32)
    ends = jnp.sum(jnp.where(order[None, :] <= order[:, None], lengths[None, :], 0), axis=1)
    before = ends[None, :] <= position[:, None]
    starts = jnp.sum(jnp.where(before, lengths[None, :], 0), axis=1)
    offsets = position - starts
    half = HD // 2
    freqs = THETA ** (-(jnp.arange(half, dtype=jnp.float32) * 2.0 / HD))
    angles = offsets.astype(jnp.float32)[:, None] * freqs[None, :]
    cosine, sine = jnp.cos(angles), jnp.sin(angles)
    return (
        offsets[:, None],
        jnp.concatenate([cosine, cosine], axis=-1),
        jnp.concatenate([-sine, sine], axis=-1),
    )


def kernel(
    spans,
    sections,
    reach,
    tok_ref,
    off_ref,
    cos_ref,
    sin_ref,
    gain_ref,
    wq_ref,
    wk_ref,
    wv_ref,
    wo_ref,
    out_ref,
    wq,
    wk,
    wv,
    wo,
    hid,
    normed,
    queries,
    kv,
    att,
    bias,
    w_sem,
    kv_send,
    kv_recv,
    hid_send,
    hid_recv,
):
    me = lax.axis_index("ctx")
    seg = lax.axis_index("pp")
    rows, width = tok_ref.shape
    groups, part = wq.shape[0], wq.shape[2]
    chunks, piece = hid.shape[0], hid.shape[2]
    kv_width = wk.shape[1]
    heads_in = part // HD

    loads = [
        pltpu.make_async_copy(wk_ref, wk, w_sem.at[0]),
        pltpu.make_async_copy(wv_ref, wv, w_sem.at[1]),
    ]
    for g in range(groups):
        loads.append(
            pltpu.make_async_copy(wq_ref.at[:, pl.ds(g * part, part)], wq.at[g], w_sem.at[2 + g])
        )
    for c in range(chunks):
        loads.append(
            pltpu.make_async_copy(
                wo_ref.at[:, pl.ds(c * piece, piece)], wo.at[c], w_sem.at[2 + groups + c]
            )
        )
    for load in loads:
        load.start()

    barrier = pltpu.get_barrier_semaphore()
    partners = []
    for d in range(1, reach + 1):
        partners.append((me >= d, {"ctx": me - d}))
        partners.append((me + d < spans, {"ctx": me + d}))
    partners.append((seg >= 1, {"pp": seg - 1}))
    partners.append((seg + 1 < sections, {"pp": seg + 1}))
    for there, where in partners:

        @pl.when(there)
        def _(where=where):
            pl.semaphore_signal(barrier, inc=1, device_id=where, device_id_type=MESH)

    for d in range(1, reach + 1):

        @pl.when(me < d)
        def _(d=d):
            kv[reach - d] = jnp.zeros(kv.shape[1:], kv.dtype)

    offset = off_ref[...]
    row = lax.broadcasted_iota(jnp.int32, (rows, rows), 0)
    col = lax.broadcasted_iota(jnp.int32, (rows, rows), 1)
    for d in range(reach + 1):
        gap = row - col + d * rows
        bias[:, pl.ds((reach - d) * rows, rows)] = jnp.where(
            (gap >= 0) & (gap <= offset), 0.0, NEG_LARGE
        )

    peers = sum(there.astype(jnp.int32) for there, where in partners)
    pl.semaphore_wait(barrier, peers)

    def hand_over(c, device):
        return pltpu.make_async_remote_copy(
            src_ref=out_ref.at[:, pl.ds(c * piece, piece)],
            dst_ref=hid.at[c],
            send_sem=hid_send.at[c],
            recv_sem=hid_recv.at[c],
            device_id={"pp": device},
            device_id_type=MESH,
        )

    def spread(d, device):
        return pltpu.make_async_remote_copy(
            src_ref=kv.at[reach],
            dst_ref=kv.at[reach - d],
            send_sem=kv_send.at[d - 1],
            recv_sem=kv_recv.at[d - 1],
            device_id={"ctx": device},
            device_id_type=MESH,
        )

    @pl.when(seg == 0)
    def _():
        for c in range(chunks):
            hid[c] = tok_ref[:, c * piece : (c + 1) * piece]

    @pl.when(seg >= 1)
    def _():
        for c in range(chunks):
            hand_over(c, seg - 1).wait_recv()

    square = jnp.zeros((rows, 1), jnp.float32)
    for c in range(chunks):
        wide = hid[c].astype(jnp.float32)
        square += jnp.sum(wide * wide, axis=-1, keepdims=True)
    inverse = lax.rsqrt(square / width + EPSILON)
    for c in range(chunks):
        at = slice(c * piece, (c + 1) * piece)
        gain = gain_ref[:, at].astype(jnp.float32)
        normed[:, at] = (hid[c].astype(jnp.float32) * inverse * gain).astype(jnp.bfloat16)

    def turn(head):
        return (head * cos_ref[...] + pltpu.roll(head, HD // 2, 1) * sin_ref[...]).astype(
            jnp.bfloat16
        )

    loads[0].wait()
    keys = jnp.dot(normed[...], wk[...], preferred_element_type=jnp.float32)
    for g in range(groups):
        kv[reach, :, g * HD : (g + 1) * HD] = turn(keys[:, g * HD : (g + 1) * HD])
    loads[1].wait()
    kv[reach, :, kv_width : 2 * kv_width] = jnp.dot(
        normed[...], wv[...], preferred_element_type=jnp.float32
    ).astype(jnp.bfloat16)

    for d in range(1, reach + 1):

        @pl.when(me + d < spans)
        def _(d=d):
            spread(d, me + d).start()

    for g in range(groups):
        loads[2 + g].wait()

    @pl.loop(0, groups)
    def _(g):
        block = jnp.dot(normed[...], wq[g], preferred_element_type=jnp.float32)
        for j in range(heads_in):
            queries[g, j * rows : (j + 1) * rows] = turn(block[:, j * HD : (j + 1) * HD])

    for d in range(1, reach + 1):

        @pl.when(me >= d)
        def _(d=d):
            spread(d, me - d).wait_recv()

    count = (reach + 1) * rows

    @pl.loop(0, groups)
    def _(g):
        k_at = pl.ds(pl.multiple_of(g * HD, HD), HD)
        v_at = pl.ds(pl.multiple_of(kv_width + g * HD, HD), HD)
        ks = kv[:, :, k_at].reshape(count, HD)
        vs = kv[:, :, v_at].reshape(count, HD)
        for j in range(heads_in):
            scores = lax.dot_general(
                queries[g, j * rows : (j + 1) * rows],
                ks,
                (((1,), (1,)), ((), ())),
                preferred_element_type=jnp.float32,
            )
            scores = scores * (HD ** (-0.5)) + bias[...]
            peak = jnp.max(scores, axis=-1, keepdims=True)
            weights = jnp.exp(scores - peak)
            total = jnp.sum(weights, axis=-1, keepdims=True)
            mixed = jnp.dot(weights.astype(jnp.bfloat16), vs, preferred_element_type=jnp.float32)
            at = pl.ds(pl.multiple_of(g * part + j * HD, HD), HD)
            att[:, at] = (mixed / total).astype(jnp.bfloat16)

    for c in range(chunks):
        loads[2 + groups + c].wait()

    @pl.loop(0, chunks)
    def _(c):
        at = pl.ds(pl.multiple_of(c * piece, piece), piece)
        out_ref[:, at] = (
            hid[c].astype(jnp.float32)
            + jnp.dot(att[...], wo[c], preferred_element_type=jnp.float32)
        ).astype(jnp.bfloat16)

        @pl.when(seg + 1 < sections)
        def _():
            pltpu.make_async_remote_copy(
                src_ref=out_ref.at[:, at],
                dst_ref=hid.at[c],
                send_sem=hid_send.at[c],
                recv_sem=hid_recv.at[c],
                device_id={"pp": seg + 1},
                device_id_type=MESH,
            ).start()

    for d in range(1, reach + 1):

        @pl.when(me + d < spans)
        def _(d=d):
            spread(d, me + d).wait_send()

    @pl.when(seg + 1 < sections)
    def _():
        for c in range(chunks):
            hand_over(c, seg + 1).wait_send()


def solution(mesh):
    spans, sections = mesh.shape["ctx"], mesh.shape["pp"]
    reach = spans // 2

    def per_device(tokens, doc_lengths, norm_gain, w_query, w_key, w_value, w_output):
        rows, width = tokens.shape[1:]
        kv_width = w_key.shape[2]
        groups = kv_width // HD
        part = w_query.shape[2] // groups
        mixed_width = w_output.shape[1]
        chunks = 4
        piece = width // chunks
        position = lax.axis_index("ctx") * rows + jnp.arange(rows, dtype=jnp.int32)
        offsets, cosine, sine = tables(position, doc_lengths)
        vmem = pl.BlockSpec(memory_space=pltpu.VMEM)
        hbm = pl.BlockSpec(memory_space=pl.ANY)
        out = pl.pallas_call(
            functools.partial(kernel, spans, sections, reach),
            out_shape=jax.ShapeDtypeStruct((rows, width), jnp.bfloat16),
            in_specs=[vmem] * 5 + [hbm] * 4,
            out_specs=vmem,
            scratch_shapes=[
                pltpu.VMEM((groups, width, part), jnp.bfloat16),
                pltpu.VMEM((width, kv_width), jnp.bfloat16),
                pltpu.VMEM((width, kv_width), jnp.bfloat16),
                pltpu.VMEM((chunks, mixed_width, piece), jnp.bfloat16),
                pltpu.VMEM((chunks, rows, piece), jnp.bfloat16),
                pltpu.VMEM((rows, width), jnp.bfloat16),
                pltpu.VMEM((groups, part // HD * rows, HD), jnp.bfloat16),
                pltpu.VMEM((reach + 1, rows, 2 * kv_width), jnp.bfloat16),
                pltpu.VMEM((rows, mixed_width), jnp.bfloat16),
                pltpu.VMEM((rows, (reach + 1) * rows), jnp.float32),
                pltpu.SemaphoreType.DMA((2 + groups + chunks,)),
                pltpu.SemaphoreType.DMA((reach,)),
                pltpu.SemaphoreType.DMA((reach,)),
                pltpu.SemaphoreType.DMA((chunks,)),
                pltpu.SemaphoreType.DMA((chunks,)),
            ],
            compiler_params=pltpu.CompilerParams(
                collective_id=0, has_side_effects=True, vmem_limit_bytes=52 << 20
            ),
        )(
            tokens[0],
            offsets,
            cosine,
            sine,
            norm_gain,
            w_query[0],
            w_key[0],
            w_value[0],
            w_output[0],
        )
        return out[None, None]

    in_specs = (
        P(None, "ctx", None),
        P(),
        P("pp", None),
        P("pp", None, None),
        P("pp", None, None),
        P("pp", None, None),
        P("pp", None, None),
    )
    return jax.shard_map(
        per_device,
        mesh=mesh,
        in_specs=in_specs,
        out_specs=P("pp", None, "ctx", None),
        check_vma=False,
    )
```

```python
import functools

import jax
import jax.numpy as jnp
from jax import lax
from jax.experimental import pallas as pl
from jax.experimental.pallas import tpu as pltpu
from jax.sharding import PartitionSpec as P

HD = 128
THETA = 500000.0
EPSILON = 1e-05
NEG_LARGE = -1e30
MESH = pl.DeviceIdType.MESH


def tables(position, lengths):
    order = jnp.arange(lengths.shape[0], dtype=jnp.int32)
    ends = jnp.sum(jnp.where(order[None, :] <= order[:, None], lengths[None, :], 0), axis=1)
    before = ends[None, :] <= position[:, None]
    starts = jnp.sum(jnp.where(before, lengths[None, :], 0), axis=1)
    offsets = position - starts
    half = HD // 2
    freqs = THETA ** (-(jnp.arange(half, dtype=jnp.float32) * 2.0 / HD))
    angles = offsets.astype(jnp.float32)[:, None] * freqs[None, :]
    cosine, sine = jnp.cos(angles), jnp.sin(angles)
    return (
        offsets[:, None],
        jnp.concatenate([cosine, cosine], axis=-1),
        jnp.concatenate([-sine, sine], axis=-1),
    )


def kernel(
    spans,
    sections,
    reach,
    tok_ref,
    off_ref,
    cos_ref,
    sin_ref,
    gain_ref,
    wq_ref,
    wk_ref,
    wv_ref,
    wo_ref,
    out_ref,
    wq,
    wk,
    wv,
    wo,
    hid,
    normed,
    queries,
    kv,
    att,
    bias,
    w_sem,
    far_send,
    near_send,
    kv_recv,
    hid_send,
    hid_recv,
):
    me = lax.axis_index("ctx")
    seg = lax.axis_index("pp")
    rows, width = tok_ref.shape
    groups, part = wq.shape[0], wq.shape[2]
    chunks, piece = hid.shape[0], hid.shape[2]
    heads_in = part // HD

    loads = [
        pltpu.make_async_copy(wk_ref, wk, w_sem.at[0]),
        pltpu.make_async_copy(wv_ref, wv, w_sem.at[1]),
    ]
    for g in range(groups):
        loads.append(
            pltpu.make_async_copy(wq_ref.at[:, pl.ds(g * part, part)], wq.at[g], w_sem.at[2 + g])
        )
    for c in range(chunks):
        loads.append(
            pltpu.make_async_copy(
                wo_ref.at[:, pl.ds(c * piece, piece)], wo.at[c], w_sem.at[2 + groups + c]
            )
        )
    for load in loads:
        load.start()

    barrier = pltpu.get_barrier_semaphore()
    partners = []
    even = lax.rem(me, 2) == 0
    pair = me + 1 - 2 * lax.rem(me, 2)
    partners.append((me >= 2, {"ctx": me - 2}))
    partners.append((me + 2 < spans, {"ctx": me + 2}))
    partners.append((me >= 0, {"ctx": pair}))
    partners.append((seg >= 1, {"pp": seg - 1}))
    partners.append((seg + 1 < sections, {"pp": seg + 1}))
    for there, where in partners:

        @pl.when(there)
        def _(where=where):
            pl.semaphore_signal(barrier, inc=1, device_id=where, device_id_type=MESH)

    for d in range(1, reach + 1):

        @pl.when(me < d)
        def _(d=d):
            for t in range(2):
                kv[t, reach - d] = jnp.zeros(kv.shape[2:], kv.dtype)

    offset = off_ref[...]
    row = lax.broadcasted_iota(jnp.int32, (rows, rows), 0)
    col = lax.broadcasted_iota(jnp.int32, (rows, rows), 1)
    for d in range(reach + 1):
        gap = row - col + d * rows
        bias[:, pl.ds((reach - d) * rows, rows)] = jnp.where(
            (gap >= 0) & (gap <= offset), 0.0, NEG_LARGE
        )

    peers = sum(there.astype(jnp.int32) for there, where in partners)
    pl.semaphore_wait(barrier, peers)

    def hand_over(c, device):
        return pltpu.make_async_remote_copy(
            src_ref=out_ref.at[:, pl.ds(c * piece, piece)],
            dst_ref=hid.at[c],
            send_sem=hid_send.at[c],
            recv_sem=hid_recv.at[c],
            device_id={"pp": device},
            device_id_type=MESH,
        )

    def along(t, d, device):
        return pltpu.make_async_remote_copy(
            src_ref=kv.at[t, reach - d],
            dst_ref=kv.at[t, reach - d - 2],
            send_sem=far_send.at[t, d // 2],
            recv_sem=kv_recv.at[t, d + 1],
            device_id={"ctx": device},
            device_id_type=MESH,
        )

    def across(t, d, to):
        return pltpu.make_async_remote_copy(
            src_ref=kv.at[t, reach - d],
            dst_ref=kv.at[t, reach - to],
            send_sem=near_send.at[t, d // 2],
            recv_sem=kv_recv.at[t, to - 1],
            device_id={"ctx": pair},
            device_id_type=MESH,
        )

    def routes(d):
        held = me >= d
        found = []
        if d + 2 <= reach:
            found.append((held & (me + 2 < spans), lambda t: along(t, d, me + 2)))
        if d + 1 <= reach:
            found.append((held & even, lambda t: across(t, d, d + 1)))
        if d >= 2:
            found.append((held & jnp.logical_not(even), lambda t: across(t, d, d - 1)))
        return found

    def pass_on(t, d):
        for open_, copy in routes(d):

            @pl.when(open_)
            def _(copy=copy):
                copy(t).start()

    @pl.when(seg == 0)
    def _():
        for c in range(chunks):
            hid[c] = tok_ref[:, c * piece : (c + 1) * piece]

    @pl.when(seg >= 1)
    def _():
        for c in range(chunks):
            hand_over(c, seg - 1).wait_recv()

    square = jnp.zeros((rows, 1), jnp.float32)
    for c in range(chunks):
        wide = hid[c].astype(jnp.float32)
        square += jnp.sum(wide * wide, axis=-1, keepdims=True)
    inverse = lax.rsqrt(square / width + EPSILON)
    for c in range(chunks):
        at = slice(c * piece, (c + 1) * piece)
        gain = gain_ref[:, at].astype(jnp.float32)
        normed[:, at] = (hid[c].astype(jnp.float32) * inverse * gain).astype(jnp.bfloat16)

    def turn(head):
        return (head * cos_ref[...] + pltpu.roll(head, HD // 2, 1) * sin_ref[...]).astype(
            jnp.bfloat16
        )

    loads[0].wait()
    keys = jnp.dot(normed[...], wk[...], preferred_element_type=jnp.float32)
    for g in range(groups):
        kv[0, reach, :, g * HD : (g + 1) * HD] = turn(keys[:, g * HD : (g + 1) * HD])
    pass_on(0, 0)
    loads[1].wait()
    kv[1, reach] = jnp.dot(
        normed[...], wv[...], preferred_element_type=jnp.float32
    ).astype(jnp.bfloat16)

    pass_on(1, 0)

    for g in range(groups):
        loads[2 + g].wait()

    @pl.loop(0, groups)
    def _(g):
        block = jnp.dot(normed[...], wq[g], preferred_element_type=jnp.float32)
        for j in range(heads_in):
            queries[g, j * rows : (j + 1) * rows] = turn(block[:, j * HD : (j + 1) * HD])

    for d in range(2, reach + 1, 2):
        for t in range(2):

            @pl.when(me >= d)
            def _(d=d, t=t):
                along(t, d - 2, me - 2).wait_recv()

            pass_on(t, d)

    for d in range(1, reach + 1, 2):
        for t in range(2):

            @pl.when(me >= d)
            def _(d=d, t=t):
                across(t, d - 1, d).wait_recv()

    count = (reach + 1) * rows

    @pl.loop(0, groups)
    def _(g):
        k_at = pl.ds(pl.multiple_of(g * HD, HD), HD)
        ks = kv[0, :, :, k_at].reshape(count, HD)
        vs = kv[1, :, :, k_at].reshape(count, HD)
        for j in range(heads_in):
            scores = lax.dot_general(
                queries[g, j * rows : (j + 1) * rows],
                ks,
                (((1,), (1,)), ((), ())),
                preferred_element_type=jnp.float32,
            )
            scores = scores * (HD ** (-0.5)) + bias[...]
            peak = jnp.max(scores, axis=-1, keepdims=True)
            weights = jnp.exp(scores - peak)
            total = jnp.sum(weights, axis=-1, keepdims=True)
            mixed = jnp.dot(weights.astype(jnp.bfloat16), vs, preferred_element_type=jnp.float32)
            at = pl.ds(pl.multiple_of(g * part + j * HD, HD), HD)
            att[:, at] = (mixed / total).astype(jnp.bfloat16)

    for c in range(chunks):
        loads[2 + groups + c].wait()

    @pl.loop(0, chunks)
    def _(c):
        at = pl.ds(pl.multiple_of(c * piece, piece), piece)
        out_ref[:, at] = (
            hid[c].astype(jnp.float32)
            + jnp.dot(att[...], wo[c], preferred_element_type=jnp.float32)
        ).astype(jnp.bfloat16)

        @pl.when(seg + 1 < sections)
        def _():
            pltpu.make_async_remote_copy(
                src_ref=out_ref.at[:, at],
                dst_ref=hid.at[c],
                send_sem=hid_send.at[c],
                recv_sem=hid_recv.at[c],
                device_id={"pp": seg + 1},
                device_id_type=MESH,
            ).start()

    for d in range(0, reach + 1, 2):
        for t in range(2):
            for open_, copy in routes(d):

                @pl.when(open_)
                def _(copy=copy, t=t):
                    copy(t).wait_send()

    @pl.when(seg + 1 < sections)
    def _():
        for c in range(chunks):
            hand_over(c, seg + 1).wait_send()


def solution(mesh):
    spans, sections = mesh.shape["ctx"], mesh.shape["pp"]
    reach = spans // 2

    def per_device(tokens, doc_lengths, norm_gain, w_query, w_key, w_value, w_output):
        rows, width = tokens.shape[1:]
        kv_width = w_key.shape[2]
        groups = kv_width // HD
        part = w_query.shape[2] // groups
        mixed_width = w_output.shape[1]
        chunks = 4
        piece = width // chunks
        position = lax.axis_index("ctx") * rows + jnp.arange(rows, dtype=jnp.int32)
        offsets, cosine, sine = tables(position, doc_lengths)
        vmem = pl.BlockSpec(memory_space=pltpu.VMEM)
        hbm = pl.BlockSpec(memory_space=pl.ANY)
        out = pl.pallas_call(
            functools.partial(kernel, spans, sections, reach),
            out_shape=jax.ShapeDtypeStruct((rows, width), jnp.bfloat16),
            in_specs=[vmem] * 5 + [hbm] * 4,
            out_specs=vmem,
            scratch_shapes=[
                pltpu.VMEM((groups, width, part), jnp.bfloat16),
                pltpu.VMEM((width, kv_width), jnp.bfloat16),
                pltpu.VMEM((width, kv_width), jnp.bfloat16),
                pltpu.VMEM((chunks, mixed_width, piece), jnp.bfloat16),
                pltpu.VMEM((chunks, rows, piece), jnp.bfloat16),
                pltpu.VMEM((rows, width), jnp.bfloat16),
                pltpu.VMEM((groups, part // HD * rows, HD), jnp.bfloat16),
                pltpu.VMEM((2, reach + 1, rows, kv_width), jnp.bfloat16),
                pltpu.VMEM((rows, mixed_width), jnp.bfloat16),
                pltpu.VMEM((rows, (reach + 1) * rows), jnp.float32),
                pltpu.SemaphoreType.DMA((2 + groups + chunks,)),
                pltpu.SemaphoreType.DMA((2, reach // 2 + 1)),
                pltpu.SemaphoreType.DMA((2, reach // 2 + 1)),
                pltpu.SemaphoreType.DMA((2, reach)),
                pltpu.SemaphoreType.DMA((chunks,)),
                pltpu.SemaphoreType.DMA((chunks,)),
            ],
            compiler_params=pltpu.CompilerParams(
                collective_id=0, has_side_effects=True, vmem_limit_bytes=52 << 20
            ),
        )(
            tokens[0],
            offsets,
            cosine,
            sine,
            norm_gain,
            w_query[0],
            w_key[0],
            w_value[0],
            w_output[0],
        )
        return out[None, None]

    in_specs = (
        P(None, "ctx", None),
        P(),
        P("pp", None),
        P("pp", None, None),
        P("pp", None, None),
        P("pp", None, None),
        P("pp", None, None),
    )
    return jax.shard_map(
        per_device,
        mesh=mesh,
        in_specs=in_specs,
        out_specs=P("pp", None, "ctx", None),
        check_vma=False,
    )
```

```python
import functools

import jax
import jax.numpy as jnp
from jax import lax
from jax.experimental import pallas as pl
from jax.experimental.pallas import tpu as pltpu
from jax.sharding import PartitionSpec as P

HD = 128
THETA = 500000.0
EPSILON = 1e-05
NEG_LARGE = -1e30
MESH = pl.DeviceIdType.MESH


def tables(position, lengths):
    order = jnp.arange(lengths.shape[0], dtype=jnp.int32)
    ends = jnp.sum(jnp.where(order[None, :] <= order[:, None], lengths[None, :], 0), axis=1)
    before = ends[None, :] <= position[:, None]
    starts = jnp.sum(jnp.where(before, lengths[None, :], 0), axis=1)
    offsets = position - starts
    half = HD // 2
    freqs = THETA ** (-(jnp.arange(half, dtype=jnp.float32) * 2.0 / HD))
    angles = offsets.astype(jnp.float32)[:, None] * freqs[None, :]
    cosine, sine = jnp.cos(angles), jnp.sin(angles)
    return (
        offsets[:, None],
        jnp.concatenate([cosine, cosine], axis=-1),
        jnp.concatenate([-sine, sine], axis=-1),
    )


def kernel(
    spans,
    sections,
    reach,
    tok_ref,
    off_ref,
    cos_ref,
    sin_ref,
    gain_ref,
    wq_ref,
    wk_ref,
    wv_ref,
    wo_ref,
    out_ref,
    wq,
    wk,
    wv,
    wo,
    hid,
    normed,
    queries,
    kv,
    att,
    bias,
    peaks,
    totals,
    sums,
    w_sem,
    far_send,
    near_send,
    kv_recv,
    hid_send,
    hid_recv,
):
    me = lax.axis_index("ctx")
    seg = lax.axis_index("pp")
    rows, width = tok_ref.shape
    groups, part = wq.shape[0], wq.shape[2]
    chunks, piece = hid.shape[0], hid.shape[2]
    heads_in = part // HD

    loads = [
        pltpu.make_async_copy(wk_ref, wk, w_sem.at[0]),
        pltpu.make_async_copy(wv_ref, wv, w_sem.at[1]),
    ]
    for g in range(groups):
        loads.append(
            pltpu.make_async_copy(wq_ref.at[:, pl.ds(g * part, part)], wq.at[g], w_sem.at[2 + g])
        )
    for c in range(chunks):
        loads.append(
            pltpu.make_async_copy(
                wo_ref.at[:, pl.ds(c * piece, piece)], wo.at[c], w_sem.at[2 + groups + c]
            )
        )
    for load in loads[:2]:
        load.start()

    barrier = pltpu.get_barrier_semaphore()
    partners = []
    even = lax.rem(me, 2) == 0
    pair = me + 1 - 2 * lax.rem(me, 2)
    partners.append((me >= 2, {"ctx": me - 2}))
    partners.append((me + 2 < spans, {"ctx": me + 2}))
    partners.append((me >= 0, {"ctx": pair}))
    partners.append((seg >= 1, {"pp": seg - 1}))
    partners.append((seg + 1 < sections, {"pp": seg + 1}))
    for there, where in partners:

        @pl.when(there)
        def _(where=where):
            pl.semaphore_signal(barrier, inc=1, device_id=where, device_id_type=MESH)

    for d in range(1, reach + 1):

        @pl.when(me < d)
        def _(d=d):
            for t in range(2):
                kv[t, reach - d] = jnp.zeros(kv.shape[2:], kv.dtype)

    offset = off_ref[...]
    row = lax.broadcasted_iota(jnp.int32, (rows, rows), 0)
    col = lax.broadcasted_iota(jnp.int32, (rows, rows), 1)
    for d in range(reach + 1):
        gap = row - col + d * rows
        bias[:, pl.ds((reach - d) * rows, rows)] = jnp.where(
            (gap >= 0) & (gap <= offset), 0.0, NEG_LARGE
        )

    peers = sum(there.astype(jnp.int32) for there, where in partners)
    pl.semaphore_wait(barrier, peers)

    def hand_over(c, device):
        return pltpu.make_async_remote_copy(
            src_ref=out_ref.at[:, pl.ds(c * piece, piece)],
            dst_ref=hid.at[c],
            send_sem=hid_send.at[c],
            recv_sem=hid_recv.at[c],
            device_id={"pp": device},
            device_id_type=MESH,
        )

    def along(t, d, device):
        return pltpu.make_async_remote_copy(
            src_ref=kv.at[t, reach - d],
            dst_ref=kv.at[t, reach - d - 2],
            send_sem=far_send.at[t, d // 2],
            recv_sem=kv_recv.at[t, d + 1],
            device_id={"ctx": device},
            device_id_type=MESH,
        )

    def across(t, d, to):
        return pltpu.make_async_remote_copy(
            src_ref=kv.at[t, reach - d],
            dst_ref=kv.at[t, reach - to],
            send_sem=near_send.at[t, d // 2],
            recv_sem=kv_recv.at[t, to - 1],
            device_id={"ctx": pair},
            device_id_type=MESH,
        )

    def routes(d):
        held = me >= d
        found = []
        if d + 2 <= reach:
            found.append((held & (me + 2 < spans), lambda t: along(t, d, me + 2)))
        if d + 1 <= reach:
            found.append((held & even, lambda t: across(t, d, d + 1)))
        if d >= 2:
            found.append((held & jnp.logical_not(even), lambda t: across(t, d, d - 1)))
        return found

    def pass_on(t, d):
        for open_, copy in routes(d):

            @pl.when(open_)
            def _(copy=copy):
                copy(t).start()

    for load in loads[2 : 2 + groups]:
        load.start()

    @pl.when(seg >= 1)
    def _():
        for load in loads[2 + groups :]:
            load.start()

    @pl.when(seg == 0)
    def _():
        for c in range(chunks):
            hid[c] = tok_ref[:, c * piece : (c + 1) * piece]

    @pl.when(seg >= 1)
    def _():
        for c in range(chunks):
            hand_over(c, seg - 1).wait_recv()

    square = jnp.zeros((rows, 1), jnp.float32)
    for c in range(chunks):
        wide = hid[c].astype(jnp.float32)
        square += jnp.sum(wide * wide, axis=-1, keepdims=True)
    inverse = lax.rsqrt(square / width + EPSILON)
    for c in range(chunks):
        at = slice(c * piece, (c + 1) * piece)
        gain = gain_ref[:, at].astype(jnp.float32)
        normed[:, at] = (hid[c].astype(jnp.float32) * inverse * gain).astype(jnp.bfloat16)

    def turn(head):
        return (head * cos_ref[...] + pltpu.roll(head, HD // 2, 1) * sin_ref[...]).astype(
            jnp.bfloat16
        )

    loads[0].wait()
    keys = jnp.dot(normed[...], wk[...], preferred_element_type=jnp.float32)
    for g in range(groups):
        kv[0, reach, :, g * HD : (g + 1) * HD] = turn(keys[:, g * HD : (g + 1) * HD])
    pass_on(0, 0)
    loads[1].wait()

    @pl.when(seg == 0)
    def _():
        for load in loads[2 + groups :]:
            load.start()

    kv[1, reach] = jnp.dot(
        normed[...], wv[...], preferred_element_type=jnp.float32
    ).astype(jnp.bfloat16)

    pass_on(1, 0)

    for g in range(groups):
        loads[2 + g].wait()

    @pl.loop(0, groups)
    def _(g):
        block = jnp.dot(normed[...], wq[g], preferred_element_type=jnp.float32)
        for j in range(heads_in):
            queries[g, j * rows : (j + 1) * rows] = turn(block[:, j * HD : (j + 1) * HD])

    def relay(d, side):
        for t in range(2):

            @pl.when(side & (me >= d))
            def _(t=t):
                along(t, d - 2, me - 2).wait_recv()
                pass_on(t, d)

    def from_pair(d):
        for t in range(2):

            @pl.when(me >= d)
            def _(t=t):
                across(t, d - 1, d).wait_recv()

    def part_of(g, j, first, last):
        at = pl.ds(pl.multiple_of(g * HD, HD), HD)
        count = (last - first) * rows
        scores = lax.dot_general(
            queries[g, j * rows : (j + 1) * rows],
            kv[0, first:last, :, at].reshape(count, HD),
            (((1,), (1,)), ((), ())),
            preferred_element_type=jnp.float32,
        )
        scores = scores * (HD ** (-0.5)) + bias[:, first * rows : last * rows]
        return scores, kv[1, first:last, :, at].reshape(count, HD)

    near = reach - 2
    relay(2, me >= 0)
    for d in range(4, reach + 1, 2):
        relay(d, jnp.logical_not(even))
    from_pair(1)

    @pl.loop(0, groups)
    def _(g):
        for j in range(heads_in):
            scores, vs = part_of(g, j, near, reach + 1)
            peak = jnp.max(scores, axis=-1, keepdims=True)
            weights = jnp.exp(scores - peak)
            total = jnp.sum(weights, axis=-1, keepdims=True)
            at = slice(j * rows, (j + 1) * rows)
            peaks[g, at] = jnp.broadcast_to(peak, (rows, HD))
            totals[g, at] = jnp.broadcast_to(total, (rows, HD))
            sums[g, at] = jnp.dot(
                weights.astype(jnp.bfloat16), vs, preferred_element_type=jnp.float32
            )

    for d in range(4, reach + 1, 2):
        relay(d, even)
    for d in range(3, reach + 1, 2):
        from_pair(d)

    @pl.loop(0, groups)
    def _(g):
        for j in range(heads_in):
            scores, vs = part_of(g, j, 0, near)
            at = slice(j * rows, (j + 1) * rows)
            old = peaks[g, at]
            peak = jnp.maximum(old[:, :1], jnp.max(scores, axis=-1, keepdims=True))
            weights = jnp.exp(scores - peak)
            fade = jnp.exp(old - peak)
            total = totals[g, at] * fade + jnp.sum(weights, axis=-1, keepdims=True)
            mixed = sums[g, at] * fade + jnp.dot(
                weights.astype(jnp.bfloat16), vs, preferred_element_type=jnp.float32
            )
            to = pl.ds(pl.multiple_of(g * part + j * HD, HD), HD)
            att[:, to] = (mixed / total).astype(jnp.bfloat16)

    for c in range(chunks):
        loads[2 + groups + c].wait()

    @pl.loop(0, chunks)
    def _(c):
        at = pl.ds(pl.multiple_of(c * piece, piece), piece)
        out_ref[:, at] = (
            hid[c].astype(jnp.float32)
            + jnp.dot(att[...], wo[c], preferred_element_type=jnp.float32)
        ).astype(jnp.bfloat16)

        @pl.when(seg + 1 < sections)
        def _():
            pltpu.make_async_remote_copy(
                src_ref=out_ref.at[:, at],
                dst_ref=hid.at[c],
                send_sem=hid_send.at[c],
                recv_sem=hid_recv.at[c],
                device_id={"pp": seg + 1},
                device_id_type=MESH,
            ).start()

    for d in range(0, reach + 1, 2):
        for t in range(2):
            for open_, copy in routes(d):

                @pl.when(open_)
                def _(copy=copy, t=t):
                    copy(t).wait_send()

    @pl.when(seg + 1 < sections)
    def _():
        for c in range(chunks):
            hand_over(c, seg + 1).wait_send()


def solution(mesh):
    spans, sections = mesh.shape["ctx"], mesh.shape["pp"]
    reach = spans // 2

    def per_device(tokens, doc_lengths, norm_gain, w_query, w_key, w_value, w_output):
        rows, width = tokens.shape[1:]
        kv_width = w_key.shape[2]
        groups = kv_width // HD
        part = w_query.shape[2] // groups
        mixed_width = w_output.shape[1]
        chunks = 4
        piece = width // chunks
        position = lax.axis_index("ctx") * rows + jnp.arange(rows, dtype=jnp.int32)
        offsets, cosine, sine = tables(position, doc_lengths)
        vmem = pl.BlockSpec(memory_space=pltpu.VMEM)
        hbm = pl.BlockSpec(memory_space=pl.ANY)
        out = pl.pallas_call(
            functools.partial(kernel, spans, sections, reach),
            out_shape=jax.ShapeDtypeStruct((rows, width), jnp.bfloat16),
            in_specs=[vmem] * 5 + [hbm] * 4,
            out_specs=vmem,
            scratch_shapes=[
                pltpu.VMEM((groups, width, part), jnp.bfloat16),
                pltpu.VMEM((width, kv_width), jnp.bfloat16),
                pltpu.VMEM((width, kv_width), jnp.bfloat16),
                pltpu.VMEM((chunks, mixed_width, piece), jnp.bfloat16),
                pltpu.VMEM((chunks, rows, piece), jnp.bfloat16),
                pltpu.VMEM((rows, width), jnp.bfloat16),
                pltpu.VMEM((groups, part // HD * rows, HD), jnp.bfloat16),
                pltpu.VMEM((2, reach + 1, rows, kv_width), jnp.bfloat16),
                pltpu.VMEM((rows, mixed_width), jnp.bfloat16),
                pltpu.VMEM((rows, (reach + 1) * rows), jnp.float32),
                pltpu.VMEM((groups, part // HD * rows, HD), jnp.float32),
                pltpu.VMEM((groups, part // HD * rows, HD), jnp.float32),
                pltpu.VMEM((groups, part // HD * rows, HD), jnp.float32),
                pltpu.SemaphoreType.DMA((2 + groups + chunks,)),
                pltpu.SemaphoreType.DMA((2, reach // 2 + 1)),
                pltpu.SemaphoreType.DMA((2, reach // 2 + 1)),
                pltpu.SemaphoreType.DMA((2, reach)),
                pltpu.SemaphoreType.DMA((chunks,)),
                pltpu.SemaphoreType.DMA((chunks,)),
            ],
            compiler_params=pltpu.CompilerParams(
                collective_id=0, has_side_effects=True, vmem_limit_bytes=52 << 20
            ),
        )(
            tokens[0],
            offsets,
            cosine,
            sine,
            norm_gain,
            w_query[0],
            w_key[0],
            w_value[0],
            w_output[0],
        )
        return out[None, None]

    in_specs = (
        P(None, "ctx", None),
        P(),
        P("pp", None),
        P("pp", None, None),
        P("pp", None, None),
        P("pp", None, None),
        P("pp", None, None),
    )
    return jax.shard_map(
        per_device,
        mesh=mesh,
        in_specs=in_specs,
        out_specs=P("pp", None, "ctx", None),
        check_vma=False,
    )
```

```python
import functools

import jax
import jax.numpy as jnp
from jax import lax
from jax.experimental import pallas as pl
from jax.experimental.pallas import tpu as pltpu
from jax.sharding import PartitionSpec as P

HD = 128
THETA = 500000.0
EPSILON = 1e-05
NEG_LARGE = -1e30
MESH = pl.DeviceIdType.MESH


def tables(position, lengths):
    order = jnp.arange(lengths.shape[0], dtype=jnp.int32)
    ends = jnp.sum(jnp.where(order[None, :] <= order[:, None], lengths[None, :], 0), axis=1)
    before = ends[None, :] <= position[:, None]
    starts = jnp.sum(jnp.where(before, lengths[None, :], 0), axis=1)
    offsets = position - starts
    half = HD // 2
    freqs = THETA ** (-(jnp.arange(half, dtype=jnp.float32) * 2.0 / HD))
    angles = offsets.astype(jnp.float32)[:, None] * freqs[None, :]
    cosine, sine = jnp.cos(angles), jnp.sin(angles)
    return (
        offsets[:, None],
        jnp.concatenate([cosine, cosine], axis=-1),
        jnp.concatenate([-sine, sine], axis=-1),
    )


def kernel(
    spans,
    sections,
    reach,
    tok_ref,
    off_ref,
    cos_ref,
    sin_ref,
    gain_ref,
    wq_ref,
    wk_ref,
    wv_ref,
    wo_ref,
    out_ref,
    wq,
    wk,
    wv,
    wo,
    hid,
    normed,
    queries,
    kv,
    att,
    bias,
    w_sem,
    far_send,
    near_send,
    kv_recv,
    hid_send,
    hid_recv,
):
    me = lax.axis_index("ctx")
    seg = lax.axis_index("pp")
    rows, width = tok_ref.shape
    groups, part = wq.shape[0], wq.shape[2]
    chunks, piece = hid.shape[0], hid.shape[2]
    heads_in = part // HD

    loads = [
        pltpu.make_async_copy(wk_ref, wk, w_sem.at[0]),
        pltpu.make_async_copy(wv_ref, wv, w_sem.at[1]),
    ]
    for g in range(groups):
        loads.append(
            pltpu.make_async_copy(wq_ref.at[:, pl.ds(g * part, part)], wq.at[g], w_sem.at[2 + g])
        )
    for c in range(chunks):
        loads.append(
            pltpu.make_async_copy(
                wo_ref.at[:, pl.ds(c * piece, piece)], wo.at[c], w_sem.at[2 + groups + c]
            )
        )
    for load in loads:
        load.start()

    barrier = pltpu.get_barrier_semaphore()
    partners = []
    even = lax.rem(me, 2) == 0
    pair = me + 1 - 2 * lax.rem(me, 2)
    partners.append((me >= 2, {"ctx": me - 2}))
    partners.append((me + 2 < spans, {"ctx": me + 2}))
    partners.append((me >= 0, {"ctx": pair}))
    partners.append((seg >= 1, {"pp": seg - 1}))
    partners.append((seg + 1 < sections, {"pp": seg + 1}))
    for there, where in partners:

        @pl.when(there)
        def _(where=where):
            pl.semaphore_signal(barrier, inc=1, device_id=where, device_id_type=MESH)

    for d in range(1, reach + 1):

        @pl.when(me < d)
        def _(d=d):
            for t in range(2):
                kv[t, reach - d] = jnp.zeros(kv.shape[2:], kv.dtype)

    offset = off_ref[...]
    row = lax.broadcasted_iota(jnp.int32, (rows, rows), 0)
    col = lax.broadcasted_iota(jnp.int32, (rows, rows), 1)
    for d in range(reach + 1):
        gap = row - col + d * rows
        bias[:, pl.ds((reach - d) * rows, rows)] = jnp.where(
            (gap >= 0) & (gap <= offset), 0.0, NEG_LARGE
        )

    peers = sum(there.astype(jnp.int32) for there, where in partners)
    pl.semaphore_wait(barrier, peers)

    def hand_over(c, device):
        return pltpu.make_async_remote_copy(
            src_ref=out_ref.at[:, pl.ds(c * piece, piece)],
            dst_ref=hid.at[c],
            send_sem=hid_send.at[c],
            recv_sem=hid_recv.at[c],
            device_id={"pp": device},
            device_id_type=MESH,
        )

    def along(t, d, device):
        return pltpu.make_async_remote_copy(
            src_ref=kv.at[t, reach - d],
            dst_ref=kv.at[t, reach - d - 2],
            send_sem=far_send.at[t, d // 2],
            recv_sem=kv_recv.at[t, d + 1],
            device_id={"ctx": device},
            device_id_type=MESH,
        )

    def across(t, d, to):
        return pltpu.make_async_remote_copy(
            src_ref=kv.at[t, reach - d],
            dst_ref=kv.at[t, reach - to],
            send_sem=near_send.at[t, d // 2],
            recv_sem=kv_recv.at[t, to - 1],
            device_id={"ctx": pair},
            device_id_type=MESH,
        )

    def routes(d):
        held = me >= d
        found = []
        if d + 2 <= reach:
            found.append((held & (me + 2 < spans), lambda t: along(t, d, me + 2)))
        if d + 1 <= reach:
            found.append((held & even, lambda t: across(t, d, d + 1)))
        if d >= 2:
            found.append((held & jnp.logical_not(even), lambda t: across(t, d, d - 1)))
        return found

    def pass_on(t, d):
        for open_, copy in routes(d):

            @pl.when(open_)
            def _(copy=copy):
                copy(t).start()

    @pl.when(seg == 0)
    def _():
        for c in range(chunks):
            hid[c] = tok_ref[:, c * piece : (c + 1) * piece]

    @pl.when(seg >= 1)
    def _():
        for c in range(chunks):
            hand_over(c, seg - 1).wait_recv()

    square = jnp.zeros((rows, 1), jnp.float32)
    for c in range(chunks):
        wide = hid[c].astype(jnp.float32)
        square += jnp.sum(wide * wide, axis=-1, keepdims=True)
    inverse = lax.rsqrt(square / width + EPSILON)
    for c in range(chunks):
        at = slice(c * piece, (c + 1) * piece)
        gain = gain_ref[:, at].astype(jnp.float32)
        normed[:, at] = (hid[c].astype(jnp.float32) * inverse * gain).astype(jnp.bfloat16)

    def turn(head):
        return (head * cos_ref[...] + pltpu.roll(head, HD // 2, 1) * sin_ref[...]).astype(
            jnp.bfloat16
        )

    loads[0].wait()
    keys = jnp.dot(normed[...], wk[...], preferred_element_type=jnp.float32)
    for g in range(groups):
        kv[0, reach, :, g * HD : (g + 1) * HD] = turn(keys[:, g * HD : (g + 1) * HD])
    pass_on(0, 0)
    loads[1].wait()
    kv[1, reach] = jnp.dot(
        normed[...], wv[...], preferred_element_type=jnp.float32
    ).astype(jnp.bfloat16)

    pass_on(1, 0)

    for g in range(groups):
        loads[2 + g].wait()

    @pl.loop(0, groups)
    def _(g):
        block = jnp.dot(normed[...], wq[g], preferred_element_type=jnp.float32)
        for j in range(heads_in):
            queries[g, j * rows : (j + 1) * rows] = turn(block[:, j * HD : (j + 1) * HD])

    for d in range(2, reach + 1, 2):
        for t in range(2):

            @pl.when(me >= d)
            def _(d=d, t=t):
                along(t, d - 2, me - 2).wait_recv()

            pass_on(t, d)

    for d in range(1, reach + 1, 2):
        for t in range(2):

            @pl.when(me >= d)
            def _(d=d, t=t):
                across(t, d - 1, d).wait_recv()

    count = (reach + 1) * rows

    for g in range(groups):
        at = slice(g * HD, (g + 1) * HD)
        ks = kv[0, :, :, at].reshape(count, HD)
        vs = kv[1, :, :, at].reshape(count, HD)
        scores = lax.dot_general(
            queries[g], ks, (((1,), (1,)), ((), ())), preferred_element_type=jnp.float32
        )
        scores = scores.reshape(heads_in, rows, count) * (HD ** (-0.5)) + bias[...][None]
        scores = scores.reshape(heads_in * rows, count)
        peak = jnp.max(scores, axis=-1, keepdims=True)
        weights = jnp.exp(scores - peak)
        total = jnp.sum(weights, axis=-1, keepdims=True)
        mixed = jnp.dot(weights.astype(jnp.bfloat16), vs, preferred_element_type=jnp.float32)
        mixed = (mixed / total).astype(jnp.bfloat16)
        for j in range(heads_in):
            to = g * part + j * HD
            att[:, to : to + HD] = mixed[j * rows : (j + 1) * rows]

    for c in range(chunks):
        loads[2 + groups + c].wait()

    @pl.loop(0, chunks)
    def _(c):
        at = pl.ds(pl.multiple_of(c * piece, piece), piece)
        out_ref[:, at] = (
            hid[c].astype(jnp.float32)
            + jnp.dot(att[...], wo[c], preferred_element_type=jnp.float32)
        ).astype(jnp.bfloat16)

        @pl.when(seg + 1 < sections)
        def _():
            pltpu.make_async_remote_copy(
                src_ref=out_ref.at[:, at],
                dst_ref=hid.at[c],
                send_sem=hid_send.at[c],
                recv_sem=hid_recv.at[c],
                device_id={"pp": seg + 1},
                device_id_type=MESH,
            ).start()

    for d in range(0, reach + 1, 2):
        for t in range(2):
            for open_, copy in routes(d):

                @pl.when(open_)
                def _(copy=copy, t=t):
                    copy(t).wait_send()

    @pl.when(seg + 1 < sections)
    def _():
        for c in range(chunks):
            hand_over(c, seg + 1).wait_send()


def solution(mesh):
    spans, sections = mesh.shape["ctx"], mesh.shape["pp"]
    reach = spans // 2

    def per_device(tokens, doc_lengths, norm_gain, w_query, w_key, w_value, w_output):
        rows, width = tokens.shape[1:]
        kv_width = w_key.shape[2]
        groups = kv_width // HD
        part = w_query.shape[2] // groups
        mixed_width = w_output.shape[1]
        chunks = 4
        piece = width // chunks
        position = lax.axis_index("ctx") * rows + jnp.arange(rows, dtype=jnp.int32)
        offsets, cosine, sine = tables(position, doc_lengths)
        vmem = pl.BlockSpec(memory_space=pltpu.VMEM)
        hbm = pl.BlockSpec(memory_space=pl.ANY)
        out = pl.pallas_call(
            functools.partial(kernel, spans, sections, reach),
            out_shape=jax.ShapeDtypeStruct((rows, width), jnp.bfloat16),
            in_specs=[vmem] * 5 + [hbm] * 4,
            out_specs=vmem,
            scratch_shapes=[
                pltpu.VMEM((groups, width, part), jnp.bfloat16),
                pltpu.VMEM((width, kv_width), jnp.bfloat16),
                pltpu.VMEM((width, kv_width), jnp.bfloat16),
                pltpu.VMEM((chunks, mixed_width, piece), jnp.bfloat16),
                pltpu.VMEM((chunks, rows, piece), jnp.bfloat16),
                pltpu.VMEM((rows, width), jnp.bfloat16),
                pltpu.VMEM((groups, part // HD * rows, HD), jnp.bfloat16),
                pltpu.VMEM((2, reach + 1, rows, kv_width), jnp.bfloat16),
                pltpu.VMEM((rows, mixed_width), jnp.bfloat16),
                pltpu.VMEM((rows, (reach + 1) * rows), jnp.float32),
                pltpu.SemaphoreType.DMA((2 + groups + chunks,)),
                pltpu.SemaphoreType.DMA((2, reach // 2 + 1)),
                pltpu.SemaphoreType.DMA((2, reach // 2 + 1)),
                pltpu.SemaphoreType.DMA((2, reach)),
                pltpu.SemaphoreType.DMA((chunks,)),
                pltpu.SemaphoreType.DMA((chunks,)),
            ],
            compiler_params=pltpu.CompilerParams(
                collective_id=0, has_side_effects=True, vmem_limit_bytes=52 << 20
            ),
        )(
            tokens[0],
            offsets,
            cosine,
            sine,
            norm_gain,
            w_query[0],
            w_key[0],
            w_value[0],
            w_output[0],
        )
        return out[None, None]

    in_specs = (
        P(None, "ctx", None),
        P(),
        P("pp", None),
        P("pp", None, None),
        P("pp", None, None),
        P("pp", None, None),
        P("pp", None, None),
    )
    return jax.shard_map(
        per_device,
        mesh=mesh,
        in_specs=in_specs,
        out_specs=P("pp", None, "ctx", None),
        check_vma=False,
    )
```
